32 devices in a mesh: group: 2 (over y), dp: 16 (over z, x, core).
Axes of the slice: x: 2, y: 2, z: 4, core: 2. Of those that a mesh axis runs over, the one named last changes fastest.
Arguments:
- clips_feat: bfloat16 [4096, 4096], P(('group', 'dp')), parts along dimension 0, may hold values from -6 to 6
- weight: bfloat16 [4096, 384], P('dp'), may hold values from -0.09375 to 0.09375
- sentences: bfloat16 [4096, 384], P(('group', 'dp')), parts along dimension 0, may hold values from -6 to 6
- log_scale: float32 [1], replicated, may hold values from 4.3 to 4.6
- bias: float32 [1], replicated, may hold values from -14 to -11
- positives: int32 [4096, 2], P(('group', 'dp')), parts along dimension 0, may hold values from 0 to 2047
Outputs:
- clip_loss: float32 [4096], P(('group', 'dp')), parts along dimension 0
- grad_weight: float32 [8192, 384], P(('group', 'dp')), parts along dimension 0
- grad_scalars: float32 [4], P('group'), parts along dimension 0
The draws below stay inside these ranges and needn't reach their ends.
There are 2 independent parts, one for each index of `group`. The reference program is written for one: setup_inputs(seed, part) draws one part's arguments, and reference() takes and returns one part's arrays. A program takes and returns all parts, laid end to end along the dimension named above; an argument that names none is the same for every part. Nothing has to cross between parts.
Inputs may be any that keep to these rules, and one draw needn't show every extreme that they name: `positives`: two sentence ids for each clip; they may coincide.
All inputs are finite; a program needn't handle non-finite values.
Results may differ from the reference program's by a relative error of at most 0.002.
The reference program's roundings to bfloat16 on the way count: a program that leaves them out, or rounds other values in their place, can miss the bound.
Values may be sent and summed in bfloat16 or wider, within the bound.
A program may use at most 64 MiB of HBM per device.

```python
import math
import jax
import jax.numpy as jnp
from jax import lax

F = 4096
E = 384
NC = 2048
NS = 2048


def set_ends(drawn, stream_key, least, largest):
    shape = drawn.shape
    spot = [jax.random.randint(jax.random.fold_in(stream_key, axis), (), 0, shape[axis]) for axis in range(len(shape))]
    drawn = drawn.at[tuple(spot)].set(least)
    longest = shape.index(max(shape))
    spot[longest] = (spot[longest] + 1) % shape[longest]
    return drawn.at[tuple(spot)].set(largest)


def shard_levels(stream_key, extent, shards, least, largest):
    level, own = 1.0, jax.random.fold_in(stream_key, 6)
    for axis_at, blocks in shards:
        draws = jnp.exp(jax.random.uniform(jax.random.fold_in(own, axis_at), (blocks,), jnp.float32, least / len(shards), largest / len(shards)))
        level = level * jnp.repeat(draws, extent[axis_at] // blocks).reshape([-1 if axis == axis_at else 1 for axis in range(len(extent))])
    return level


def normal_values(stream_key, extent, scale, bound, pieces=(), held_as=jnp.bfloat16):
    array = jax.random.normal(stream_key, extent, jnp.float32) * scale
    if len(pieces) > 0:
        array = shard_levels(stream_key, extent, pieces, -0.22, 0.18) * array
    return jnp.clip(array, min=-bound, max=bound).astype(held_as)


def setup_inputs(seed: int = 0, part: int = 0) -> dict:
    key_list = jax.random.split(jax.random.key(seed), 7)
    own_keys = jax.random.split(jax.random.fold_in(key_list[6], part), 7)
    return {
        "clips_feat": normal_values(own_keys[0], (NC, F), 1.0, 6.0, ((0, 16),)),
        "weight": normal_values(key_list[1], (F, E), F ** -0.5, 0.09375, ((0, 16),)),
        "sentences": normal_values(own_keys[2], (NS, E), 1.0, 6.0, ((0, 16),)),
        "log_scale": jnp.clip(jax.random.uniform(key_list[3], (1,), jnp.float32, 4.3, 4.6), 4.3, 4.6),
        "bias": jnp.clip(jax.random.uniform(key_list[4], (1,), jnp.float32, -14.0, -11.0), -14.0, -11.0),
        "positives": set_ends(jax.random.randint(own_keys[5], (NC, 2), 0, NS), jax.random.fold_in(own_keys[5], 1), 0, NS - 1).astype(jnp.int32),
    }


def reference(clips_feat, weight, sentences, log_scale, bias, positives):
    total_clips = clips_feat.shape[0]
    total_sent = sentences.shape[0]
    embed_width = weight.shape[1]
    proj = jnp.dot(clips_feat, weight, preferred_element_type=jnp.float32)
    inverse = lax.rsqrt(lax.optimization_barrier(jnp.sum(proj * proj, axis=1, keepdims=True)) + 1e-06)
    unit32 = proj * inverse
    clip_unit = unit32.astype(jnp.bfloat16)
    sent32 = sentences.astype(jnp.float32)
    sent_unit = (sent32 * lax.rsqrt(lax.optimization_barrier(jnp.sum(sent32 * sent32, axis=1, keepdims=True)) + 1e-06)).astype(jnp.bfloat16)
    scale = jnp.exp(log_scale[0])
    shift = bias[0]
    columns = jnp.arange(total_sent, dtype=jnp.int32)
    block_rows = math.gcd(total_clips, 512)
    clip_blocks = clip_unit.reshape(total_clips // block_rows, block_rows, embed_width)
    pos_blocks = positives.reshape(total_clips // block_rows, block_rows, 2)

    def one_block(inputs):
        units, pairs = inputs
        products = jnp.dot(units, sent_unit.T, preferred_element_type=jnp.float32)
        logits = scale * products + shift
        matched = (pairs[:, 0:1] == columns[None, :]) | (pairs[:, 1:2] == columns[None, :])
        target = jnp.where(matched, jnp.float32(1.0), jnp.float32(-1.0))
        margin = target * logits
        losses = -lax.optimization_barrier(jnp.sum(jax.nn.log_sigmoid(margin), axis=1))
        grad_logit = -target * jax.nn.sigmoid(-margin) / total_clips
        dscale = jnp.sum(grad_logit * (scale * products))
        dbias = jnp.sum(grad_logit)
        grad = jnp.dot(grad_logit.astype(jnp.bfloat16), sent_unit, preferred_element_type=jnp.float32)
        return (losses, grad, dscale, dbias)
    losses, grads, dscales, dbiases = lax.map(one_block, (clip_blocks, pos_blocks))
    clip_loss = losses.reshape(total_clips)
    grad_unit = scale * grads.reshape(total_clips, embed_width)
    inner = lax.optimization_barrier(jnp.sum(unit32 * grad_unit, axis=1, keepdims=True))
    grad_proj = (inverse * (grad_unit - unit32 * inner)).astype(jnp.bfloat16)
    grad_weight = jnp.dot(clips_feat.T, grad_proj, preferred_element_type=jnp.float32)
    grad_scalars = jnp.stack([jnp.sum(dscales), jnp.sum(dbiases)])
    return (clip_loss, grad_weight, grad_scalars)
```

```python
import functools

import jax
import jax.numpy as jnp
from jax import lax
from jax.experimental import pallas as pl
from jax.experimental.pallas import tpu as pltpu
from jax.sharding import PartitionSpec as P

MESH = pl.DeviceIdType.MESH
TAIL = 16


def fused(n, clips_ref, w_ref, s_ref, ls_ref, bias_ref, pos_ref, loss_ref, gw_ref, sc_ref,
          wfull, sfull, gfull, cturn, cfull, proj_acc,
          w_send, w_recv, s_send, s_recv, g_send, g_recv, c_send, c_recv):
    rows, width = s_ref.shape
    depth = w_ref.shape[0]
    group = lax.axis_index("group")
    me = lax.axis_index("dp")
    z = me // 4
    x = (me // 2) % 2
    c = me % 2
    mid = (z * (3 - z)) // 2
    near = z + 1 - 2 * (z % 2)
    across = 3 - z
    far = (z + 2) % 4
    zs = [z, near, mid * across + (1 - mid) * far, mid * far + (1 - mid) * across]

    def at(zz, xx, cc):
        return zz * 4 + xx * 2 + cc

    barrier = pltpu.get_barrier_semaphore()
    for k in range(1, n):
        pl.semaphore_signal(barrier, inc=1, device_id=(group, lax.rem(me + k, n)), device_id_type=MESH)

    wfull[me] = w_ref[...]
    s32 = s_ref[...].astype(jnp.float32)
    sfull[me] = (s32 * lax.rsqrt(jnp.sum(s32 * s32, axis=1, keepdims=True) + 1e-06)).astype(jnp.bfloat16)
    pl.semaphore_wait(barrier, n - 1)

    def block_copy(buf, send, recv, origin, target, k):
        return pltpu.make_async_remote_copy(
            src_ref=buf.at[origin], dst_ref=buf.at[origin], send_sem=send.at[k],
            recv_sem=recv.at[origin], device_id=(group, target), device_id_type=MESH)

    z_out = at(near, x, c)
    z_mid = at(across, x, c)
    x_out = at(z, 1 - x, c)
    c_out = at(z, x, 1 - c)
    W = (wfull, w_send, w_recv)
    S = (sfull, s_send, s_recv)
    G = (gfull, g_send, g_recv)

    def z_step(array, i):
        buf, send, recv = array
        origin = at(zs[i], x, c)
        if i > 0:
            block_copy(buf, send, recv, origin, me + 1 - 2 * c, 0).wait_recv()
        if i == 0:
            block_copy(buf, send, recv, origin, z_out, 0).start()
        if i < 2:
            @pl.when(mid == 1)
            def _():
                block_copy(buf, send, recv, origin, z_mid, 1 + i).start()
        else:
            @pl.when(mid == 1)
            def _():
                block_copy(buf, send, recv, origin, z_out, 1 + i).start()
        block_copy(buf, send, recv, origin, x_out, 5 + i).start()
        block_copy(buf, send, recv, origin, c_out, 9 + i).start()
        return origin

    def x_step(array, i):
        buf, send, recv = array
        origin = at(zs[i], 1 - x, c)
        block_copy(buf, send, recv, origin, c_out, 0).wait_recv()
        block_copy(buf, send, recv, origin, c_out, 13 + i).start()
        return origin

    def c_step(array, i, xx):
        buf, send, recv = array
        origin = at(zs[i], xx, 1 - c)
        block_copy(buf, send, recv, origin, c_out, 0).wait_recv()
        return origin

    def drain(array):
        buf, send, recv = array
        for k in range(17):
            if 1 <= k <= 4:
                @pl.when(mid == 1)
                def _():
                    block_copy(buf, send, recv, me, c_out, k).wait_send()
            else:
                block_copy(buf, send, recv, me, c_out, k).wait_send()

    proj_acc[...] = jnp.zeros_like(proj_acc)

    def project(origin):
        columns = pl.ds(pl.multiple_of(origin * depth, depth), depth)
        proj_acc[...] += jnp.dot(clips_ref[:, columns], wfull[origin], preferred_element_type=jnp.float32)

    def turn_copy(k):
        target = lax.rem(me + k, n)
        mine = pl.ds(pl.multiple_of(me * rows, rows), rows)
        return pltpu.make_async_remote_copy(
            src_ref=cturn.at[target], dst_ref=cfull.at[:, mine], send_sem=c_send.at[k],
            recv_sem=c_recv.at[k], device_id=(group, target), device_id_type=MESH)

    def turn(k):
        target = lax.rem(me + k, n)
        columns = pl.ds(pl.multiple_of(target * depth, depth), depth)
        block = clips_ref[:, columns].T
        if k == 0:
            cfull[:, pl.ds(pl.multiple_of(me * rows, rows), rows)] = block
        else:
            cturn[target] = block

    z_step(W, 0)
    z_step(S, 0)
    project(me)
    for k in range(n):
        turn(k)
    for i in range(1, 4):
        origin = z_step(W, i)
        z_step(S, i)
        project(origin)
    for k in range(1, n):
        turn_copy(k).start()
    for i in range(4):
        origin = x_step(W, i)
        x_step(S, i)
        project(origin)
    for i in range(4):
        project(c_step(W, i, x))
        c_step(S, i, x)
    for i in range(4):
        project(c_step(W, i, 1 - x))
        c_step(S, i, 1 - x)

    proj = proj_acc[...]
    inverse = lax.rsqrt(jnp.sum(proj * proj, axis=1, keepdims=True) + 1e-06)
    unit32 = proj * inverse
    clip_unit = unit32.astype(jnp.bfloat16)
    span = 4 * rows
    scale = jnp.exp(jnp.full((1, span), ls_ref[0], jnp.float32))
    shift = bias_ref[0]
    inv_count = 1.0 / (rows * n)
    first_pos = pos_ref[:, 0:1]
    second_pos = pos_ref[:, 1:2]
    grad = jnp.zeros((rows, width), jnp.float32)
    losses = jnp.zeros((rows, 1), jnp.float32)
    dscale = jnp.zeros((1, span), jnp.float32)
    dbias = jnp.zeros((1, span), jnp.float32)
    for i in range(n // 4):
        block = sfull[4 * i:4 * i + 4].reshape(span, width)
        products = lax.dot_general(clip_unit, block, (((1,), (1,)), ((), ())), preferred_element_type=jnp.float32)
        scaled = scale * products
        logits = scaled + shift
        columns = i * span + lax.broadcasted_iota(jnp.int32, (rows, span), 1)
        matched = (first_pos == columns) | (second_pos == columns)
        margin = jnp.where(matched, logits, -logits)
        small = jnp.exp(-jnp.abs(margin))
        losses = losses + jnp.sum(jnp.maximum(-margin, 0.0) + jnp.log1p(small), axis=1, keepdims=True)
        chance = jnp.where(margin >= 0.0, small, 1.0) / (1.0 + small) * inv_count
        grad_logit = jnp.where(matched, -chance, chance)
        dscale = dscale + jnp.sum(grad_logit * scaled, axis=0, keepdims=True)
        dbias = dbias + jnp.sum(grad_logit, axis=0, keepdims=True)
        grad = grad + jnp.dot(grad_logit.astype(jnp.bfloat16), block, preferred_element_type=jnp.float32)
    grad_unit = scale[:, :width] * grad
    inner = jnp.sum(unit32 * grad_unit, axis=1, keepdims=True)
    gfull[me, :rows, :] = (inverse * (grad_unit - unit32 * inner)).astype(jnp.bfloat16)
    both = jnp.where(lax.broadcasted_iota(jnp.int32, (TAIL, width), 1) < 128,
                     jnp.sum(dscale, axis=1, keepdims=True), jnp.sum(dbias, axis=1, keepdims=True))
    high = both.astype(jnp.bfloat16)
    rest = both - high.astype(jnp.float32)
    middle = rest.astype(jnp.bfloat16)
    low = rest - middle.astype(jnp.float32)
    row = lax.broadcasted_iota(jnp.int32, (TAIL, width), 0)
    pieces = jnp.where(row == 0, high.astype(jnp.float32),
                       jnp.where(row == 1, middle.astype(jnp.float32), jnp.where(row == 2, low, 0.0)))
    gfull[me, rows:, :] = pieces.astype(jnp.bfloat16)

    z_step(G, 0)
    square = lax.broadcasted_iota(jnp.int32, (rows, rows), 0) == lax.broadcasted_iota(jnp.int32, (rows, rows), 1)
    loss_ref[...] = jnp.sum(jnp.where(square, losses, 0.0), axis=0, keepdims=True)
    for k in range(1, n):
        turn_copy(k).wait_recv()

    def weigh(origin, first=False):
        columns = pl.ds(pl.multiple_of(origin * rows, rows), rows)
        term = jnp.dot(cfull[:, columns], gfull[origin, :rows, :], preferred_element_type=jnp.float32)
        if first:
            gw_ref[...] = term
        else:
            gw_ref[...] += term

    weigh(me, True)
    for i in range(1, 4):
        weigh(z_step(G, i))
    for i in range(4):
        weigh(x_step(G, i))
    for i in range(4):
        weigh(c_step(G, i, x))
    for i in range(4):
        weigh(c_step(G, i, 1 - x))
    tails = jnp.zeros((TAIL, width), jnp.float32)
    for p in range(n):
        tails = tails + gfull[p, rows:, :].astype(jnp.float32)
    sc_ref[0] = jnp.sum(tails[:, 0:1])
    sc_ref[1] = jnp.sum(tails[:, 128:129])
    drain(W)
    drain(S)
    drain(G)
    for k in range(1, n):
        turn_copy(k).wait_send()


def in_kernel(clips_feat, weight, sentences, log_scale, bias, positives):
    n = lax.axis_size("dp")
    rows, features = clips_feat.shape
    depth, width = weight.shape
    vmem = pl.BlockSpec(memory_space=pltpu.VMEM)
    smem = pl.BlockSpec(memory_space=pltpu.SMEM)
    dma = pltpu.SemaphoreType.DMA
    loss, grad_weight, scalars = pl.pallas_call(
        functools.partial(fused, n),
        out_shape=(
            jax.ShapeDtypeStruct((1, rows), jnp.float32),
            jax.ShapeDtypeStruct((depth, width), jnp.float32),
            jax.ShapeDtypeStruct((2,), jnp.float32),
        ),
        in_specs=[vmem, vmem, vmem, smem, smem, vmem],
        out_specs=(vmem, vmem, smem),
        scratch_shapes=[
            pltpu.VMEM((n, depth, width), jnp.bfloat16),
            pltpu.VMEM((n, rows, width), jnp.bfloat16),
            pltpu.VMEM((n, rows + TAIL, width), jnp.bfloat16),
            pltpu.VMEM((n, depth, rows), jnp.bfloat16),
            pltpu.VMEM((depth, n * rows), jnp.bfloat16),
            pltpu.VMEM((rows, width), jnp.float32),
            dma((17,)), dma((n,)), dma((17,)), dma((n,)), dma((17,)), dma((n,)), dma((n,)), dma((n,)),
        ],
        compiler_params=pltpu.CompilerParams(
            collective_id=0, has_side_effects=True, vmem_limit_bytes=40 * 1024 * 1024),
        cost_estimate=pl.CostEstimate(flops=1300000000, bytes_accessed=3000000, transcendentals=1000000),
    )(clips_feat, weight, sentences, log_scale, bias, positives)
    return loss.reshape(rows), grad_weight, scalars


column_block = 2048


def swapped(x, axis, apart):
    return lax.ppermute(x, axis, [(i, i ^ 1 << apart) for i in range(lax.axis_size(axis))])


def shards(clips_feat, weight, sentences, log_scale, bias, positives):
    rows_here = clips_feat.shape[0]
    embed_width = weight.shape[1]
    devices = lax.axis_size("dp")
    position = lax.axis_index("dp")
    full_weight = lax.all_gather(weight, "dp", axis=0, tiled=True)
    proj = jnp.dot(clips_feat, full_weight, preferred_element_type=jnp.float32)
    inverse = lax.rsqrt(jnp.sum(proj * proj, axis=1, keepdims=True) + 1e-06)
    unit32 = proj * inverse
    clip_unit = unit32.astype(jnp.bfloat16)
    sent32 = sentences.astype(jnp.float32)
    sent_unit = (
        sent32 * lax.rsqrt(jnp.sum(sent32 * sent32, axis=1, keepdims=True) + 1e-06)
    ).astype(jnp.bfloat16)
    scale = jnp.exp(log_scale[0])
    shift = bias[0]
    inv_count = 1.0 / (rows_here * devices)
    first_pos = positives[:, 0:1]
    second_pos = positives[:, 1:2]

    def one_tile(carry, block, start):
        losses, grad, dscale, dbias = carry
        span = block.shape[0]
        products = lax.dot_general(
            clip_unit, block, (((1,), (1,)), ((), ())), preferred_element_type=jnp.float32
        )
        logits = scale * products + shift
        columns = start + lax.iota(jnp.int32, span)
        matched = (first_pos == columns[None, :]) | (second_pos == columns[None, :])
        target = jnp.where(matched, jnp.float32(1.0), jnp.float32(-1.0))
        margin = target * logits
        losses = losses - jnp.sum(jax.nn.log_sigmoid(margin), axis=1)
        grad_logit = -target * jax.nn.sigmoid(-margin) * inv_count
        dscale = dscale + jnp.sum(grad_logit * (scale * products))
        dbias = dbias + jnp.sum(grad_logit)
        grad = grad + jnp.dot(
            grad_logit.astype(jnp.bfloat16), block, preferred_element_type=jnp.float32
        )
        return (losses, grad, dscale, dbias)

    def tile_rows(carry, piece, start):
        span = piece.shape[0]
        if span > column_block and span % column_block == 0:
            stacked = piece.reshape(span // column_block, column_block, embed_width)
            offsets = start + column_block * lax.iota(jnp.int32, span // column_block)

            def step_once(inner_carry, inputs):
                return (one_tile(inner_carry, inputs[0], inputs[1]), None)

            result, unused = lax.scan(step_once, carry, (stacked, offsets))
            return result
        return one_tile(carry, piece, start)

    initial = (
        jnp.zeros((rows_here,), jnp.float32),
        jnp.zeros((rows_here, embed_width), jnp.float32),
        jnp.float32(0.0),
        jnp.float32(0.0),
    )
    carry = tile_rows(initial, sent_unit, position * rows_here)
    buffer = sent_unit
    levels = devices.bit_length() - 1
    for level in range(levels):
        other = swapped(buffer, "dp", level)
        stride = 1 << level
        partner_base = jnp.bitwise_xor(position, stride) // stride * stride
        carry = tile_rows(carry, other, partner_base * rows_here)
        if level + 1 < levels:
            upper = position // stride % 2 == 1
            buffer = jnp.where(
                upper,
                jnp.concatenate([other, buffer], axis=0),
                jnp.concatenate([buffer, other], axis=0),
            )
    clip_loss, grad, dscale, dbias = carry
    grad_unit = scale * grad
    inner = jnp.sum(unit32 * grad_unit, axis=1, keepdims=True)
    grad_proj = (inverse * (grad_unit - unit32 * inner)).astype(jnp.bfloat16)
    grad_weight = lax.psum_scatter(
        lax.dot_general(
            clips_feat, grad_proj, (((0,), (0,)), ((), ())), preferred_element_type=jnp.float32
        ),
        "dp",
        scatter_dimension=0,
        tiled=True,
    )
    summed = lax.psum((dscale, dbias), "dp")
    grad_scalars = jnp.stack([summed[0], summed[1]])
    return (clip_loss, grad_weight, grad_scalars)


def solution(mesh):
    in_specs = (
        P(("group", "dp"), None),
        P("dp", None),
        P(("group", "dp"), None),
        P(),
        P(),
        P(("group", "dp"), None),
    )
    out_specs = (P(("group", "dp")), P(("group", "dp"), None), P("group"))
    body = in_kernel if mesh.shape["dp"] == 16 else shards
    return jax.shard_map(body, mesh=mesh, in_specs=in_specs, out_specs=out_specs, check_vma=False)
```

```python
import functools

import jax
import jax.numpy as jnp
from jax import lax
from jax.experimental import pallas as pl
from jax.experimental.pallas import tpu as pltpu
from jax.sharding import PartitionSpec as P

MESH = pl.DeviceIdType.MESH
TAIL = 16


def fused(n, clips_hbm, w_hbm, s_hbm, ls_ref, bias_ref, pos_ref, loss_ref, gw_ref, sc_ref,
          clips_ref, s_ref, wfull, sfull, gfull, cturn, cfull, proj_acc, in_sem,
          w_send, w_recv, s_send, s_recv, g_send, g_recv, c_send, c_recv):
    rows, width = s_ref.shape
    depth = w_hbm.shape[0]
    group = lax.axis_index("group")
    me = lax.axis_index("dp")
    z = me // 4
    x = (me // 2) % 2
    c = me % 2
    mid = (z * (3 - z)) // 2
    near = z + 1 - 2 * (z % 2)
    across = 3 - z
    far = (z + 2) % 4
    zs = [z, near, mid * across + (1 - mid) * far, mid * far + (1 - mid) * across]

    def at(zz, xx, cc):
        return zz * 4 + xx * 2 + cc

    w_in = pltpu.make_async_copy(w_hbm, wfull.at[me], in_sem.at[0])
    s_in = pltpu.make_async_copy(s_hbm, s_ref, in_sem.at[1])
    clips_in = pltpu.make_async_copy(clips_hbm, clips_ref, in_sem.at[2])
    w_in.start()
    s_in.start()
    clips_in.start()
    barrier = pltpu.get_barrier_semaphore()
    for k in range(1, n):
        pl.semaphore_signal(barrier, inc=1, device_id=(group, lax.rem(me + k, n)), device_id_type=MESH)

    s_in.wait()
    s32 = s_ref[...].astype(jnp.float32)
    sfull[(x * 2 + c) * 4 + z] = (s32 * lax.rsqrt(jnp.sum(s32 * s32, axis=1, keepdims=True) + 1e-06)).astype(jnp.bfloat16)
    w_in.wait()
    pl.semaphore_wait(barrier, n - 1)

    def block_copy(buf, send, recv, origin, target, k):
        slot = sent_slot(origin) if buf is sfull else origin
        return pltpu.make_async_remote_copy(
            src_ref=buf.at[slot], dst_ref=buf.at[slot], send_sem=send.at[k],
            recv_sem=recv.at[origin], device_id=(group, target), device_id_type=MESH)

    def sent_slot(origin):
        return (origin % 4) * 4 + origin // 4

    z_out = at(near, x, c)
    z_mid = at(across, x, c)
    x_out = at(z, 1 - x, c)
    c_out = at(z, x, 1 - c)
    W = (wfull, w_send, w_recv)
    S = (sfull, s_send, s_recv)
    G = (gfull, g_send, g_recv)

    def z_step(array, i):
        buf, send, recv = array
        origin = at(zs[i], x, c)
        if i > 0:
            block_copy(buf, send, recv, origin, me + 1 - 2 * c, 0).wait_recv()
        if i == 0:
            block_copy(buf, send, recv, origin, z_out, 0).start()
        if i < 2:
            @pl.when(mid == 1)
            def _():
                block_copy(buf, send, recv, origin, z_mid, 1 + i).start()
        else:
            @pl.when(mid == 1)
            def _():
                block_copy(buf, send, recv, origin, z_out, 1 + i).start()
        block_copy(buf, send, recv, origin, x_out, 5 + i).start()
        block_copy(buf, send, recv, origin, c_out, 9 + i).start()
        return origin

    def x_step(array, i):
        buf, send, recv = array
        origin = at(zs[i], 1 - x, c)
        block_copy(buf, send, recv, origin, c_out, 0).wait_recv()
        block_copy(buf, send, recv, origin, c_out, 13 + i).start()
        return origin

    def c_step(array, i, xx):
        buf, send, recv = array
        origin = at(zs[i], xx, 1 - c)
        block_copy(buf, send, recv, origin, c_out, 0).wait_recv()
        return origin

    def drain(array):
        buf, send, recv = array
        for k in range(17):
            if 1 <= k <= 4:
                @pl.when(mid == 1)
                def _():
                    block_copy(buf, send, recv, me, c_out, k).wait_send()
            else:
                block_copy(buf, send, recv, me, c_out, k).wait_send()

    proj_acc[...] = jnp.zeros_like(proj_acc)

    def project(origin):
        columns = pl.ds(pl.multiple_of(origin * depth, depth), depth)
        proj_acc[...] += jnp.dot(clips_ref[:, columns], wfull[origin], preferred_element_type=jnp.float32)

    def turn_target(k):
        return at((z + k // 4) % 4, (x + (k // 2) % 2) % 2, (c + k % 2) % 2)

    def turn_copy(k):
        mine = pl.ds(pl.multiple_of(me * rows, rows), rows)
        return pltpu.make_async_remote_copy(
            src_ref=cturn.at[k], dst_ref=cfull.at[:, mine], send_sem=c_send.at[k],
            recv_sem=c_recv.at[k], device_id=(group, turn_target(k)), device_id_type=MESH)

    def turn(k):
        columns = pl.ds(pl.multiple_of(turn_target(k) * depth, depth), depth)
        block = clips_ref[:, columns].T
        if k == 0:
            cfull[:, pl.ds(pl.multiple_of(me * rows, rows), rows)] = block
        else:
            cturn[k] = block
            turn_copy(k).start()

    z_step(W, 0)
    z_step(S, 0)
    clips_in.wait()
    project(me)
    turn(0)
    project(z_step(W, 1))
    z_step(S, 1)
    project(z_step(W, 2))
    z_step(S, 2)
    project(z_step(W, 3))
    z_step(S, 3)
    turn(9)
    turn(12)
    turn(5)
    turn(8)
    turn(4)
    turn(13)
    turn(1)
    project(x_step(W, 0))
    x_step(S, 0)
    project(x_step(W, 1))
    x_step(S, 1)
    project(x_step(W, 2))
    x_step(S, 2)
    project(x_step(W, 3))
    x_step(S, 3)
    turn(10)
    turn(11)
    turn(6)
    turn(7)
    turn(14)
    turn(15)
    turn(2)
    turn(3)
    project(c_step(W, 0, x))
    project(c_step(W, 1, x))
    project(c_step(W, 2, x))
    project(c_step(W, 3, x))
    project(c_step(W, 0, 1 - x))
    project(c_step(W, 1, 1 - x))
    project(c_step(W, 2, 1 - x))
    project(c_step(W, 3, 1 - x))

    proj = proj_acc[...]
    inverse = lax.rsqrt(jnp.sum(proj * proj, axis=1, keepdims=True) + 1e-06)
    unit32 = proj * inverse
    clip_unit = unit32.astype(jnp.bfloat16)
    span = 4 * rows
    scale = jnp.exp(jnp.full((1, span), ls_ref[0], jnp.float32))
    shift = bias_ref[0]
    inv_count = 1.0 / (rows * n)
    first_pos = pos_ref[:, 0:1]
    second_pos = pos_ref[:, 1:2]
    grad = jnp.zeros((rows, width), jnp.float32)
    losses = jnp.zeros((rows, 1), jnp.float32)
    dscale = jnp.zeros((1, span), jnp.float32)
    dbias = jnp.zeros((1, span), jnp.float32)
    for xx, cc in ((x, c), (1 - x, c), (x, 1 - c), (1 - x, 1 - c)):
        if cc is not c:
            for i in range(4):
                c_step(S, i, xx)
        place = xx * 2 + cc
        block = sfull[pl.ds(place * 4, 4)].reshape(span, width)
        products = lax.dot_general(clip_unit, block, (((1,), (1,)), ((), ())), preferred_element_type=jnp.float32)
        scaled = scale * products
        logits = scaled + shift
        lane = lax.broadcasted_iota(jnp.int32, (1, span), 1)
        columns = (lane // rows * 4 + place) * rows + lane % rows
        matched = (first_pos == columns) | (second_pos == columns)
        margin = jnp.where(matched, logits, -logits)
        small = jnp.exp(-jnp.abs(margin))
        losses = losses + jnp.sum(jnp.maximum(-margin, 0.0) + jnp.log1p(small), axis=1, keepdims=True)
        chance = jnp.where(margin >= 0.0, small, 1.0) / (1.0 + small) * inv_count
        grad_logit = jnp.where(matched, -chance, chance)
        dscale = dscale + jnp.sum(grad_logit * scaled, axis=0, keepdims=True)
        dbias = dbias + jnp.sum(grad_logit, axis=0, keepdims=True)
        grad = grad + jnp.dot(grad_logit.astype(jnp.bfloat16), block, preferred_element_type=jnp.float32)
    grad_unit = scale[:, :width] * grad
    inner = jnp.sum(unit32 * grad_unit, axis=1, keepdims=True)
    gfull[me, :rows, :] = (inverse * (grad_unit - unit32 * inner)).astype(jnp.bfloat16)
    both = jnp.where(lax.broadcasted_iota(jnp.int32, (TAIL, width), 1) < 128,
                     jnp.sum(dscale, axis=1, keepdims=True), jnp.sum(dbias, axis=1, keepdims=True))
    high = both.astype(jnp.bfloat16)
    rest = both - high.astype(jnp.float32)
    middle = rest.astype(jnp.bfloat16)
    low = rest - middle.astype(jnp.float32)
    row = lax.broadcasted_iota(jnp.int32, (TAIL, width), 0)
    pieces = jnp.where(row == 0, high.astype(jnp.float32),
                       jnp.where(row == 1, middle.astype(jnp.float32), jnp.where(row == 2, low, 0.0)))
    gfull[me, rows:, :] = pieces.astype(jnp.bfloat16)

    z_step(G, 0)
    square = lax.broadcasted_iota(jnp.int32, (rows, rows), 0) == lax.broadcasted_iota(jnp.int32, (rows, rows), 1)
    loss_ref[...] = jnp.sum(jnp.where(square, losses, 0.0), axis=0, keepdims=True)
    for k in range(1, n):
        turn_copy(k).wait_recv()

    def weigh(origin, first=False):
        columns = pl.ds(pl.multiple_of(origin * rows, rows), rows)
        term = jnp.dot(cfull[:, columns], gfull[origin, :rows, :], preferred_element_type=jnp.float32)
        if first:
            gw_ref[...] = term
        else:
            gw_ref[...] += term

    weigh(me, True)
    for i in range(1, 4):
        weigh(z_step(G, i))
    for i in range(4):
        weigh(x_step(G, i))
    for i in range(4):
        weigh(c_step(G, i, x))
    for i in range(4):
        weigh(c_step(G, i, 1 - x))
    tails = jnp.zeros((TAIL, width), jnp.float32)
    for p in range(n):
        tails = tails + gfull[p, rows:, :].astype(jnp.float32)
    sc_ref[0] = jnp.sum(tails[:, 0:1])
    sc_ref[1] = jnp.sum(tails[:, 128:129])
    drain(W)
    drain(S)
    drain(G)
    for k in range(1, n):
        turn_copy(k).wait_send()


def in_kernel(clips_feat, weight, sentences, log_scale, bias, positives):
    n = lax.axis_size("dp")
    rows, features = clips_feat.shape
    depth, width = weight.shape
    vmem = pl.BlockSpec(memory_space=pltpu.VMEM)
    hbm = pl.BlockSpec(memory_space=pl.ANY)
    smem = pl.BlockSpec(memory_space=pltpu.SMEM)
    dma = pltpu.SemaphoreType.DMA
    loss, grad_weight, scalars = pl.pallas_call(
        functools.partial(fused, n),
        out_shape=(
            jax.ShapeDtypeStruct((1, rows), jnp.float32),
            jax.ShapeDtypeStruct((depth, width), jnp.float32),
            jax.ShapeDtypeStruct((2,), jnp.float32),
        ),
        in_specs=[hbm, hbm, hbm, smem, smem, vmem],
        out_specs=(vmem, vmem, smem),
        scratch_shapes=[
            pltpu.VMEM((rows, features), jnp.bfloat16),
            pltpu.VMEM((rows, width), jnp.bfloat16),
            pltpu.VMEM((n, depth, width), jnp.bfloat16),
            pltpu.VMEM((n, rows, width), jnp.bfloat16),
            pltpu.VMEM((n, rows + TAIL, width), jnp.bfloat16),
            pltpu.VMEM((n, depth, rows), jnp.bfloat16),
            pltpu.VMEM((depth, n * rows), jnp.bfloat16),
            pltpu.VMEM((rows, width), jnp.float32),
            dma((3,)), dma((17,)), dma((n,)), dma((17,)), dma((n,)), dma((17,)), dma((n,)), dma((n,)), dma((n,)),
        ],
        compiler_params=pltpu.CompilerParams(
            collective_id=0, has_side_effects=True, vmem_limit_bytes=40 * 1024 * 1024),
        cost_estimate=pl.CostEstimate(flops=1300000000, bytes_accessed=3000000, transcendentals=1000000),
    )(clips_feat, weight, sentences, log_scale, bias, positives)
    return loss.reshape(rows), grad_weight, scalars


column_block = 2048


def swapped(x, axis, apart):
    return lax.ppermute(x, axis, [(i, i ^ 1 << apart) for i in range(lax.axis_size(axis))])


def shards(clips_feat, weight, sentences, log_scale, bias, positives):
    rows_here = clips_feat.shape[0]
    embed_width = weight.shape[1]
    devices = lax.axis_size("dp")
    position = lax.axis_index("dp")
    full_weight = lax.all_gather(weight, "dp", axis=0, tiled=True)
    proj = jnp.dot(clips_feat, full_weight, preferred_element_type=jnp.float32)
    inverse = lax.rsqrt(jnp.sum(proj * proj, axis=1, keepdims=True) + 1e-06)
    unit32 = proj * inverse
    clip_unit = unit32.astype(jnp.bfloat16)
    sent32 = sentences.astype(jnp.float32)
    sent_unit = (
        sent32 * lax.rsqrt(jnp.sum(sent32 * sent32, axis=1, keepdims=True) + 1e-06)
    ).astype(jnp.bfloat16)
    scale = jnp.exp(log_scale[0])
    shift = bias[0]
    inv_count = 1.0 / (rows_here * devices)
    first_pos = positives[:, 0:1]
    second_pos = positives[:, 1:2]

    def one_tile(carry, block, start):
        losses, grad, dscale, dbias = carry
        span = block.shape[0]
        products = lax.dot_general(
            clip_unit, block, (((1,), (1,)), ((), ())), preferred_element_type=jnp.float32
        )
        logits = scale * products + shift
        columns = start + lax.iota(jnp.int32, span)
        matched = (first_pos == columns[None, :]) | (second_pos == columns[None, :])
        target = jnp.where(matched, jnp.float32(1.0), jnp.float32(-1.0))
        margin = target * logits
        losses = losses - jnp.sum(jax.nn.log_sigmoid(margin), axis=1)
        grad_logit = -target * jax.nn.sigmoid(-margin) * inv_count
        dscale = dscale + jnp.sum(grad_logit * (scale * products))
        dbias = dbias + jnp.sum(grad_logit)
        grad = grad + jnp.dot(
            grad_logit.astype(jnp.bfloat16), block, preferred_element_type=jnp.float32
        )
        return (losses, grad, dscale, dbias)

    def tile_rows(carry, piece, start):
        span = piece.shape[0]
        if span > column_block and span % column_block == 0:
            stacked = piece.reshape(span // column_block, column_block, embed_width)
            offsets = start + column_block * lax.iota(jnp.int32, span // column_block)

            def step_once(inner_carry, inputs):
                return (one_tile(inner_carry, inputs[0], inputs[1]), None)

            result, unused = lax.scan(step_once, carry, (stacked, offsets))
            return result
        return one_tile(carry, piece, start)

    initial = (
        jnp.zeros((rows_here,), jnp.float32),
        jnp.zeros((rows_here, embed_width), jnp.float32),
        jnp.float32(0.0),
        jnp.float32(0.0),
    )
    carry = tile_rows(initial, sent_unit, position * rows_here)
    buffer = sent_unit
    levels = devices.bit_length() - 1
    for level in range(levels):
        other = swapped(buffer, "dp", level)
        stride = 1 << level
        partner_base = jnp.bitwise_xor(position, stride) // stride * stride
        carry = tile_rows(carry, other, partner_base * rows_here)
        if level + 1 < levels:
            upper = position // stride % 2 == 1
            buffer = jnp.where(
                upper,
                jnp.concatenate([other, buffer], axis=0),
                jnp.concatenate([buffer, other], axis=0),
            )
    clip_loss, grad, dscale, dbias = carry
    grad_unit = scale * grad
    inner = jnp.sum(unit32 * grad_unit, axis=1, keepdims=True)
    grad_proj = (inverse * (grad_unit - unit32 * inner)).astype(jnp.bfloat16)
    grad_weight = lax.psum_scatter(
        lax.dot_general(
            clips_feat, grad_proj, (((0,), (0,)), ((), ())), preferred_element_type=jnp.float32
        ),
        "dp",
        scatter_dimension=0,
        tiled=True,
    )
    summed = lax.psum((dscale, dbias), "dp")
    grad_scalars = jnp.stack([summed[0], summed[1]])
    return (clip_loss, grad_weight, grad_scalars)


def solution(mesh):
    in_specs = (
        P(("group", "dp"), None),
        P("dp", None),
        P(("group", "dp"), None),
        P(),
        P(),
        P(("group", "dp"), None),
    )
    out_specs = (P(("group", "dp")), P(("group", "dp"), None), P("group"))
    body = in_kernel if mesh.shape["dp"] == 16 else shards
    return jax.shard_map(body, mesh=mesh, in_specs=in_specs, out_specs=out_specs, check_vma=False)
```

```python
import functools

import jax
import jax.numpy as jnp
from jax import lax
from jax.experimental import pallas as pl
from jax.experimental.pallas import tpu as pltpu
from jax.sharding import PartitionSpec as P

MESH = pl.DeviceIdType.MESH
TAIL = 16


def fused(n, clips_hbm, w_hbm, s_hbm, ls_ref, bias_ref, pos_ref, loss_ref, gw_ref, sc_ref,
          clips_ref, s_ref, wfull, sfull, gfull, cturn, cfull, proj_acc, in_sem,
          w_send, w_recv, s_send, s_recv, g_send, g_recv, c_send, c_recv, y_send, y_recv):
    rows, width = s_ref.shape
    depth = w_hbm.shape[0]
    group = lax.axis_index("group")
    me = lax.axis_index("dp")
    z = me // 4
    x = (me // 2) % 2
    c = me % 2
    mid = (z * (3 - z)) // 2
    near = z + 1 - 2 * (z % 2)
    across = 3 - z
    far = (z + 2) % 4
    zs = [z, near, mid * across + (1 - mid) * far, mid * far + (1 - mid) * across]

    def at(zz, xx, cc):
        return zz * 4 + xx * 2 + cc

    w_in = pltpu.make_async_copy(w_hbm, wfull.at[me], in_sem.at[0])
    s_in = pltpu.make_async_copy(s_hbm, s_ref, in_sem.at[1])
    clips_in = pltpu.make_async_copy(clips_hbm, clips_ref, in_sem.at[2])
    w_in.start()
    s_in.start()
    clips_in.start()
    barrier = pltpu.get_barrier_semaphore()
    for k in range(1, n):
        pl.semaphore_signal(barrier, inc=1, device_id=(group, lax.rem(me + k, n)), device_id_type=MESH)
    pl.semaphore_signal(barrier, inc=1, device_id=(1 - group, me), device_id_type=MESH)

    s_in.wait()
    s32 = s_ref[...].astype(jnp.float32)
    sfull[(x * 2 + c) * 4 + z] = (s32 * lax.rsqrt(jnp.sum(s32 * s32, axis=1, keepdims=True) + 1e-06)).astype(jnp.bfloat16)
    w_in.wait()
    pl.semaphore_wait(barrier, n)

    def block_copy(buf, send, recv, origin, target, k):
        slot = sent_slot(origin) if buf is sfull else origin
        return pltpu.make_async_remote_copy(
            src_ref=buf.at[slot], dst_ref=buf.at[slot], send_sem=send.at[k],
            recv_sem=recv.at[origin], device_id=(group, target), device_id_type=MESH)

    def sent_slot(origin):
        return (origin % 4) * 4 + origin // 4

    z_out = at(near, x, c)
    z_mid = at(across, x, c)
    x_out = at(z, 1 - x, c)
    c_out = at(z, x, 1 - c)
    W = (wfull, w_send, w_recv)
    S = (sfull, s_send, s_recv)
    G = (gfull, g_send, g_recv)

    half = depth // 2

    def half_copy(origin, target, k):
        part = wfull.at[origin, pl.ds(pl.multiple_of(group * half, half), half), :]
        return pltpu.make_async_remote_copy(
            src_ref=part, dst_ref=part, send_sem=w_send.at[k],
            recv_sem=w_recv.at[origin], device_id=(group, target), device_id_type=MESH)

    def twin_copy(i, which):
        origin = at(zs[i + 1], x, c) if i < 3 else at(zs[i - 3], 1 - x, c)
        part = wfull.at[origin, pl.ds(pl.multiple_of(which * half, half), half), :]
        return pltpu.make_async_remote_copy(
            src_ref=part, dst_ref=part, send_sem=y_send.at[i],
            recv_sem=y_recv.at[i], device_id=(1 - group, me), device_id_type=MESH)

    def wz_step(i):
        origin = at(zs[i], x, c)
        if i > 0:
            half_copy(origin, z_out, 0).wait_recv()
        if i == 0:
            half_copy(origin, z_out, 0).start()
        @pl.when(mid == 1)
        def _():
            half_copy(origin, z_mid if i < 2 else z_out, 1 + i).start()
        half_copy(origin, x_out, 5 + i).start()
        if i == 0:
            block_copy(wfull, w_send, w_recv, origin, c_out, 9).start()
        else:
            twin_copy(i - 1, group).start()

    def wx_step(i):
        half_copy(at(zs[i], 1 - x, c), x_out, 0).wait_recv()
        twin_copy(i + 3, group).start()

    def twin_step(i):
        origin = at(zs[i + 1], x, c) if i < 3 else at(zs[i - 3], 1 - x, c)
        twin_copy(i, 1 - group).wait_recv()
        block_copy(wfull, w_send, w_recv, origin, c_out, 10 + i).start()
        return origin

    def drain_halves():
        for k in range(9):
            if 1 <= k <= 4:
                @pl.when(mid == 1)
                def _():
                    half_copy(me, c_out, k).wait_send()
            else:
                half_copy(me, c_out, k).wait_send()
        for k in range(9, 17):
            block_copy(wfull, w_send, w_recv, me, c_out, k).wait_send()
        for i in range(7):
            twin_copy(i, group).wait_send()

    def z_step(array, i):
        buf, send, recv = array
        origin = at(zs[i], x, c)
        if i > 0:
            block_copy(buf, send, recv, origin, me + 1 - 2 * c, 0).wait_recv()
        if i == 0:
            block_copy(buf, send, recv, origin, z_out, 0).start()
        if i < 2:
            @pl.when(mid == 1)
            def _():
                block_copy(buf, send, recv, origin, z_mid, 1 + i).start()
        else:
            @pl.when(mid == 1)
            def _():
                block_copy(buf, send, recv, origin, z_out, 1 + i).start()
        block_copy(buf, send, recv, origin, x_out, 5 + i).start()
        block_copy(buf, send, recv, origin, c_out, 9 + i).start()
        return origin

    def x_step(array, i):
        buf, send, recv = array
        origin = at(zs[i], 1 - x, c)
        block_copy(buf, send, recv, origin, c_out, 0).wait_recv()
        block_copy(buf, send, recv, origin, c_out, 13 + i).start()
        return origin

    def c_step(array, i, xx):
        buf, send, recv = array
        origin = at(zs[i], xx, 1 - c)
        block_copy(buf, send, recv, origin, c_out, 0).wait_recv()
        return origin

    def drain(array):
        buf, send, recv = array
        for k in range(17):
            if 1 <= k <= 4:
                @pl.when(mid == 1)
                def _():
                    block_copy(buf, send, recv, me, c_out, k).wait_send()
            else:
                block_copy(buf, send, recv, me, c_out, k).wait_send()

    proj_acc[...] = jnp.zeros_like(proj_acc)

    def project(origin):
        columns = pl.ds(pl.multiple_of(origin * depth, depth), depth)
        proj_acc[...] += jnp.dot(clips_ref[:, columns], wfull[origin], preferred_element_type=jnp.float32)

    def turn_target(k):
        return at((z + k // 4) % 4, (x + (k // 2) % 2) % 2, (c + k % 2) % 2)

    def turn_copy(k):
        mine = pl.ds(pl.multiple_of(me * rows, rows), rows)
        return pltpu.make_async_remote_copy(
            src_ref=cturn.at[k], dst_ref=cfull.at[:, mine], send_sem=c_send.at[k],
            recv_sem=c_recv.at[k], device_id=(group, turn_target(k)), device_id_type=MESH)

    def turn(k):
        columns = pl.ds(pl.multiple_of(turn_target(k) * depth, depth), depth)
        block = clips_ref[:, columns].T
        if k == 0:
            cfull[:, pl.ds(pl.multiple_of(me * rows, rows), rows)] = block
        else:
            cturn[k] = block
            turn_copy(k).start()

    wz_step(0)
    z_step(S, 0)
    clips_in.wait()
    project(me)
    turn(0)
    wz_step(1)
    z_step(S, 1)
    wz_step(2)
    z_step(S, 2)
    wz_step(3)
    z_step(S, 3)
    turn(9)
    turn(12)
    turn(5)
    turn(8)
    turn(4)
    turn(13)
    turn(1)
    wx_step(0)
    x_step(S, 0)
    project(twin_step(0))
    wx_step(1)
    x_step(S, 1)
    project(twin_step(1))
    wx_step(2)
    x_step(S, 2)
    project(twin_step(2))
    wx_step(3)
    x_step(S, 3)
    turn(10)
    turn(11)
    turn(6)
    turn(7)
    turn(14)
    turn(15)
    turn(2)
    turn(3)
    project(twin_step(3))
    project(twin_step(4))
    project(twin_step(5))
    project(twin_step(6))
    project(c_step(W, 0, x))
    project(c_step(W, 1, x))
    project(c_step(W, 2, x))
    project(c_step(W, 3, x))
    project(c_step(W, 0, 1 - x))
    project(c_step(W, 1, 1 - x))
    project(c_step(W, 2, 1 - x))
    project(c_step(W, 3, 1 - x))

    proj = proj_acc[...]
    inverse = lax.rsqrt(jnp.sum(proj * proj, axis=1, keepdims=True) + 1e-06)
    unit32 = proj * inverse
    clip_unit = unit32.astype(jnp.bfloat16)
    span = 4 * rows
    scale = jnp.exp(jnp.full((1, span), ls_ref[0], jnp.float32))
    shift = bias_ref[0]
    inv_count = 1.0 / (rows * n)
    first_pos = pos_ref[:, 0:1]
    second_pos = pos_ref[:, 1:2]
    grad = jnp.zeros((rows, width), jnp.float32)
    losses = jnp.zeros((rows, 1), jnp.float32)
    dscale = jnp.zeros((1, span), jnp.float32)
    dbias = jnp.zeros((1, span), jnp.float32)
    for xx, cc in ((x, c), (1 - x, c), (x, 1 - c), (1 - x, 1 - c)):
        if cc is not c:
            for i in range(4):
                c_step(S, i, xx)
        place = xx * 2 + cc
        block = sfull[pl.ds(place * 4, 4)].reshape(span, width)
        products = lax.dot_general(clip_unit, block, (((1,), (1,)), ((), ())), preferred_element_type=jnp.float32)
        scaled = scale * products
        logits = scaled + shift
        lane = lax.broadcasted_iota(jnp.int32, (1, span), 1)
        columns = (lane // rows * 4 + place) * rows + lane % rows
        matched = (first_pos == columns) | (second_pos == columns)
        margin = jnp.where(matched, logits, -logits)
        small = jnp.exp(-jnp.abs(margin))
        losses = losses + jnp.sum(jnp.maximum(-margin, 0.0) + jnp.log1p(small), axis=1, keepdims=True)
        chance = jnp.where(margin >= 0.0, small, 1.0) / (1.0 + small) * inv_count
        grad_logit = jnp.where(matched, -chance, chance)
        dscale = dscale + jnp.sum(grad_logit * scaled, axis=0, keepdims=True)
        dbias = dbias + jnp.sum(grad_logit, axis=0, keepdims=True)
        grad = grad + jnp.dot(grad_logit.astype(jnp.bfloat16), block, preferred_element_type=jnp.float32)
    grad_unit = scale[:, :width] * grad
    inner = jnp.sum(unit32 * grad_unit, axis=1, keepdims=True)
    gfull[me, :rows, :] = (inverse * (grad_unit - unit32 * inner)).astype(jnp.bfloat16)
    both = jnp.where(lax.broadcasted_iota(jnp.int32, (TAIL, width), 1) < 128,
                     jnp.sum(dscale, axis=1, keepdims=True), jnp.sum(dbias, axis=1, keepdims=True))
    high = both.astype(jnp.bfloat16)
    rest = both - high.astype(jnp.float32)
    middle = rest.astype(jnp.bfloat16)
    low = rest - middle.astype(jnp.float32)
    row = lax.broadcasted_iota(jnp.int32, (TAIL, width), 0)
    pieces = jnp.where(row == 0, high.astype(jnp.float32),
                       jnp.where(row == 1, middle.astype(jnp.float32), jnp.where(row == 2, low, 0.0)))
    gfull[me, rows:, :] = pieces.astype(jnp.bfloat16)

    z_step(G, 0)
    square = lax.broadcasted_iota(jnp.int32, (rows, rows), 0) == lax.broadcasted_iota(jnp.int32, (rows, rows), 1)
    loss_ref[...] = jnp.sum(jnp.where(square, losses, 0.0), axis=0, keepdims=True)
    for k in range(1, n):
        turn_copy(k).wait_recv()

    def weigh(origin, first=False):
        columns = pl.ds(pl.multiple_of(origin * rows, rows), rows)
        term = jnp.dot(cfull[:, columns], gfull[origin, :rows, :], preferred_element_type=jnp.float32)
        if first:
            gw_ref[...] = term
        else:
            gw_ref[...] += term

    weigh(me, True)
    for i in range(1, 4):
        weigh(z_step(G, i))
    for i in range(4):
        weigh(x_step(G, i))
    for i in range(4):
        weigh(c_step(G, i, x))
    for i in range(4):
        weigh(c_step(G, i, 1 - x))
    tails = jnp.zeros((TAIL, width), jnp.float32)
    for p in range(n):
        tails = tails + gfull[p, rows:, :].astype(jnp.float32)
    sc_ref[0] = jnp.sum(tails[:, 0:1])
    sc_ref[1] = jnp.sum(tails[:, 128:129])
    drain_halves()
    drain(S)
    drain(G)
    for k in range(1, n):
        turn_copy(k).wait_send()


def in_kernel(clips_feat, weight, sentences, log_scale, bias, positives):
    n = lax.axis_size("dp")
    rows, features = clips_feat.shape
    depth, width = weight.shape
    vmem = pl.BlockSpec(memory_space=pltpu.VMEM)
    hbm = pl.BlockSpec(memory_space=pl.ANY)
    smem = pl.BlockSpec(memory_space=pltpu.SMEM)
    dma = pltpu.SemaphoreType.DMA
    loss, grad_weight, scalars = pl.pallas_call(
        functools.partial(fused, n),
        out_shape=(
            jax.ShapeDtypeStruct((1, rows), jnp.float32),
            jax.ShapeDtypeStruct((depth, width), jnp.float32),
            jax.ShapeDtypeStruct((2,), jnp.float32),
        ),
        in_specs=[hbm, hbm, hbm, smem, smem, vmem],
        out_specs=(vmem, vmem, smem),
        scratch_shapes=[
            pltpu.VMEM((rows, features), jnp.bfloat16),
            pltpu.VMEM((rows, width), jnp.bfloat16),
            pltpu.VMEM((n, depth, width), jnp.bfloat16),
            pltpu.VMEM((n, rows, width), jnp.bfloat16),
            pltpu.VMEM((n, rows + TAIL, width), jnp.bfloat16),
            pltpu.VMEM((n, depth, rows), jnp.bfloat16),
            pltpu.VMEM((depth, n * rows), jnp.bfloat16),
            pltpu.VMEM((rows, width), jnp.float32),
            dma((3,)), dma((17,)), dma((n,)), dma((17,)), dma((n,)), dma((17,)), dma((n,)), dma((n,)), dma((n,)),
            dma((7,)), dma((7,)),
        ],
        compiler_params=pltpu.CompilerParams(
            collective_id=0, has_side_effects=True, vmem_limit_bytes=40 * 1024 * 1024),
        cost_estimate=pl.CostEstimate(flops=1300000000, bytes_accessed=3000000, transcendentals=1000000),
    )(clips_feat, weight, sentences, log_scale, bias, positives)
    return loss.reshape(rows), grad_weight, scalars


column_block = 2048


def swapped(x, axis, apart):
    return lax.ppermute(x, axis, [(i, i ^ 1 << apart) for i in range(lax.axis_size(axis))])


def shards(clips_feat, weight, sentences, log_scale, bias, positives):
    rows_here = clips_feat.shape[0]
    embed_width = weight.shape[1]
    devices = lax.axis_size("dp")
    position = lax.axis_index("dp")
    full_weight = lax.all_gather(weight, "dp", axis=0, tiled=True)
    proj = jnp.dot(clips_feat, full_weight, preferred_element_type=jnp.float32)
    inverse = lax.rsqrt(jnp.sum(proj * proj, axis=1, keepdims=True) + 1e-06)
    unit32 = proj * inverse
    clip_unit = unit32.astype(jnp.bfloat16)
    sent32 = sentences.astype(jnp.float32)
    sent_unit = (
        sent32 * lax.rsqrt(jnp.sum(sent32 * sent32, axis=1, keepdims=True) + 1e-06)
    ).astype(jnp.bfloat16)
    scale = jnp.exp(log_scale[0])
    shift = bias[0]
    inv_count = 1.0 / (rows_here * devices)
    first_pos = positives[:, 0:1]
    second_pos = positives[:, 1:2]

    def one_tile(carry, block, start):
        losses, grad, dscale, dbias = carry
        span = block.shape[0]
        products = lax.dot_general(
            clip_unit, block, (((1,), (1,)), ((), ())), preferred_element_type=jnp.float32
        )
        logits = scale * products + shift
        columns = start + lax.iota(jnp.int32, span)
        matched = (first_pos == columns[None, :]) | (second_pos == columns[None, :])
        target = jnp.where(matched, jnp.float32(1.0), jnp.float32(-1.0))
        margin = target * logits
        losses = losses - jnp.sum(jax.nn.log_sigmoid(margin), axis=1)
        grad_logit = -target * jax.nn.sigmoid(-margin) * inv_count
        dscale = dscale + jnp.sum(grad_logit * (scale * products))
        dbias = dbias + jnp.sum(grad_logit)
        grad = grad + jnp.dot(
            grad_logit.astype(jnp.bfloat16), block, preferred_element_type=jnp.float32
        )
        return (losses, grad, dscale, dbias)

    def tile_rows(carry, piece, start):
        span = piece.shape[0]
        if span > column_block and span % column_block == 0:
            stacked = piece.reshape(span // column_block, column_block, embed_width)
            offsets = start + column_block * lax.iota(jnp.int32, span // column_block)

            def step_once(inner_carry, inputs):
                return (one_tile(inner_carry, inputs[0], inputs[1]), None)

            result, unused = lax.scan(step_once, carry, (stacked, offsets))
            return result
        return one_tile(carry, piece, start)

    initial = (
        jnp.zeros((rows_here,), jnp.float32),
        jnp.zeros((rows_here, embed_width), jnp.float32),
        jnp.float32(0.0),
        jnp.float32(0.0),
    )
    carry = tile_rows(initial, sent_unit, position * rows_here)
    buffer = sent_unit
    levels = devices.bit_length() - 1
    for level in range(levels):
        other = swapped(buffer, "dp", level)
        stride = 1 << level
        partner_base = jnp.bitwise_xor(position, stride) // stride * stride
        carry = tile_rows(carry, other, partner_base * rows_here)
        if level + 1 < levels:
            upper = position // stride % 2 == 1
            buffer = jnp.where(
                upper,
                jnp.concatenate([other, buffer], axis=0),
                jnp.concatenate([buffer, other], axis=0),
            )
    clip_loss, grad, dscale, dbias = carry
    grad_unit = scale * grad
    inner = jnp.sum(unit32 * grad_unit, axis=1, keepdims=True)
    grad_proj = (inverse * (grad_unit - unit32 * inner)).astype(jnp.bfloat16)
    grad_weight = lax.psum_scatter(
        lax.dot_general(
            clips_feat, grad_proj, (((0,), (0,)), ((), ())), preferred_element_type=jnp.float32
        ),
        "dp",
        scatter_dimension=0,
        tiled=True,
    )
    summed = lax.psum((dscale, dbias), "dp")
    grad_scalars = jnp.stack([summed[0], summed[1]])
    return (clip_loss, grad_weight, grad_scalars)


def solution(mesh):
    in_specs = (
        P(("group", "dp"), None),
        P("dp", None),
        P(("group", "dp"), None),
        P(),
        P(),
        P(("group", "dp"), None),
    )
    out_specs = (P(("group", "dp")), P(("group", "dp"), None), P("group"))
    body = in_kernel if mesh.shape["dp"] == 16 and mesh.shape["group"] == 2 else shards
    return jax.shard_map(body, mesh=mesh, in_specs=in_specs, out_specs=out_specs, check_vma=False)
```
